256 devices in a mesh: lat: 64 (over z, y, x_hi), wid: 4 (over x_lo, core).
Axes of the slice: x: 4 (x_hi: 2, x_lo: 2; x = x_hi * 2 + x_lo), y: 4, z: 8, core: 2. Of those that a mesh axis runs over, the one named last changes fastest.
Arguments:
- tokens: bfloat16 [2, 256, 3584], P(None, None, 'wid'), may hold values from -6 to 6
- encoder: bfloat16 [3584, 65536], P('wid', 'lat'), may hold values from -0.09375 to 0.09375
- decoder: bfloat16 [65536, 3584], P('lat', 'wid'), may hold values from -0.09375 to 0.09375
- enc_bias: float32 [65536], P('lat'), may hold values from -3 to 3
- dec_bias: float32 [3584], P('wid'), may hold values from -3 to 3
- packed_masks: int32 [2, 16, 65536], P(None, None, 'lat'), may hold values from 0 to 65535
Outputs:
- grad_encoder: float32 [3584, 65536], P('wid', 'lat')
- grad_decoder: float32 [65536, 3584], P('lat', 'wid')
- grad_enc_bias: float32 [65536], P('lat')
- grad_dec_bias: float32 [3584], P('wid')
The draws below stay inside these ranges and needn't reach their ends.
All inputs are finite; a program needn't handle non-finite values.
Results may differ from the reference program's by a relative error of at most 0.022.
Values may be sent and summed in bfloat16 or wider, within the bound.
No kernel may reach another device: no remote copies, remote signals or barrier semaphores. Data moves between devices by JAX's collectives and lax.ppermute only.
A program may use at most 64 MiB of HBM per device.

```python
import jax
import jax.numpy as jnp
from jax import lax

D = 3584
MICRO = 2
MB_TOK = 256
WORDS = 16
LATENTS = 65536
N_WID = 4


def set_ends(entries, key, low, high):
    spot = [jax.random.randint(jax.random.fold_in(key, axis), (), 0, length) for axis, length in enumerate(entries.shape)]
    widest = entries.shape.index(max(entries.shape))
    neighbour = spot[:widest] + [(spot[widest] + 1) % entries.shape[widest]] + spot[widest + 1:]
    return entries.at[tuple(spot)].set(low).at[tuple(neighbour)].set(high)


def steps_of(key, shape, shards, smallest, largest):
    level = 1.0
    for axis_at, shards_of in shards:
        draws = jax.random.uniform(jax.random.fold_in(jax.random.fold_in(key, 6), axis_at), (shards_of,), jnp.float32, smallest / len(shards), largest / len(shards))
        level = level * jnp.repeat(jnp.exp(draws), shape[axis_at] // shards_of).reshape((-1,) + (1,) * (len(shape) - 1 - axis_at))
    return level


def centred(key, extent, spread, limit, pieces=(), kind=jnp.bfloat16):
    result = jax.random.normal(key, extent, jnp.float32) * spread
    if len(pieces) > 0:
        result = steps_of(key, extent, pieces, -0.22, 0.18) * result
    return jnp.clip(result, min=-limit, max=limit).astype(kind)


def setup_inputs(seed: int = 0) -> dict:
    keys = jax.random.split(jax.random.key(seed), 7)
    return {
        "tokens": centred(keys[0], (MICRO, MB_TOK, D), 1.0, 6.0, ((2, 4),)),
        "encoder": centred(keys[1], (D, LATENTS), D ** -0.5, 0.09375, ((0, 4), (1, 64))),
        "decoder": centred(keys[2], (LATENTS, D), D ** -0.5, 0.09375, ((0, 64), (1, 4))),
        "enc_bias": centred(keys[3], (LATENTS,), 0.5, 3.0, ((0, 64),), jnp.float32),
        "dec_bias": centred(keys[4], (D,), 0.5, 3.0, ((0, 4),), jnp.float32),
        "packed_masks": set_ends(jax.random.randint(keys[5], (MICRO, WORDS, LATENTS), 0, 65536), jax.random.fold_in(keys[5], 1), 0, 65535).astype(jnp.int32),
    }


def unpack_bits(words):
    shifts = jnp.arange(16, dtype=jnp.int32)
    bits = jnp.bitwise_and(jnp.right_shift(words[:, None, :], shifts[None, :, None]), 1)
    return bits.reshape(-1, words.shape[-1]).astype(jnp.float32)


def rounded_blocks(left, right_cols, quarter):
    total = jnp.zeros((left.shape[0], right_cols.shape[1]), jnp.float32)
    for block in range(N_WID):
        span_left = left[:, block * quarter:(block + 1) * quarter]
        span_right = right_cols[block * quarter:(block + 1) * quarter, :]
        piece = jnp.dot(span_left, span_right, preferred_element_type=jnp.float32).astype(jnp.bfloat16)
        piece = lax.optimization_barrier(piece)
        total = total + piece.astype(jnp.float32)
    return total


def reference(tokens, encoder, decoder, enc_bias, dec_bias, packed_masks):
    quarter = D // N_WID
    grad_encoder = jnp.zeros(encoder.shape, jnp.float32)
    grad_decoder = jnp.zeros(decoder.shape, jnp.float32)
    grad_enc_bias = jnp.zeros(enc_bias.shape, jnp.float32)
    grad_dec_bias = jnp.zeros(dec_bias.shape, jnp.float32)
    decoder_cols = decoder.T
    for micro in range(MICRO):
        inputs_now = tokens[micro]
        gating = unpack_bits(packed_masks[micro])
        preact = enc_bias[None, :] + rounded_blocks(inputs_now, encoder, quarter)
        activity = (preact * gating).astype(jnp.bfloat16)
        residue = jnp.dot(activity, decoder, preferred_element_type=jnp.float32) + dec_bias[None, :] - inputs_now.astype(jnp.float32)
        scaled_error = (residue / MB_TOK).astype(jnp.bfloat16)
        latent_grad = rounded_blocks(scaled_error, decoder_cols, quarter)
        pre_grad = latent_grad * gating
        grad_encoder = grad_encoder + jnp.dot(inputs_now.T, pre_grad.astype(jnp.bfloat16), preferred_element_type=jnp.float32)
        grad_decoder = grad_decoder + jnp.dot(activity.T, scaled_error, preferred_element_type=jnp.float32)
        grad_enc_bias = grad_enc_bias + jnp.sum(pre_grad, axis=0)
        grad_dec_bias = grad_dec_bias + jnp.sum(residue, axis=0) / MB_TOK
    return grad_encoder, grad_decoder, grad_enc_bias, grad_dec_bias
```

```python
import jax
import jax.numpy as jnp
from jax import lax
from jax.sharding import Mesh
from jax.sharding import PartitionSpec as P

MB_TOK = 256
HALF = 128
LAT = ("z", "y", "xh")
WID = ("xl", "c")
N_LAT = 64
ROWS = MB_TOK // N_LAT
SWAP = [(0, 1), (1, 0)]
f32, bf16 = jnp.float32, jnp.bfloat16


def unpack_bits(words):
    shifts = jnp.arange(16, dtype=jnp.int32)
    bits = jnp.bitwise_and(jnp.right_shift(words[:, None, :], shifts[None, :, None]), 1)
    return bits.reshape(-1, words.shape[-1])


def own_first(halves, c):
    own = lax.dynamic_index_in_dim(halves, c, 0, keepdims=False)
    other = lax.dynamic_index_in_dim(halves, 1 - c, 0, keepdims=False)
    return own, other


def wid_sum(part):
    got = lax.ppermute(part[HALF:], "c", SWAP)
    chip = (part[:HALF].astype(f32) + got.astype(f32)).astype(bf16)
    away = lax.ppermute(chip, "xl", SWAP)
    return chip.astype(f32) + away.astype(f32)


def shards(tokens, encoder, decoder, enc_bias, dec_bias, masks):
    c = lax.axis_index("c")
    lat = lax.axis_index(LAT)
    micros = tokens.shape[0]
    toks, gates, acts, errs, pres = [], [], [], [], []
    for m in range(micros):
        own, other = own_first(tokens[m].reshape(2, HALF, -1), c)
        toks.append(jnp.concatenate([own, other], axis=0))
        words = lax.dynamic_slice_in_dim(masks[m], c * 8, 8, axis=0)
        gates.append(unpack_bits(words))
    for m in range(micros):
        part = jnp.dot(toks[m], encoder, preferred_element_type=f32).astype(bf16)
        preact = wid_sum(part) + enc_bias[None, :]
        own = jnp.where(gates[m] != 0, preact, 0.0).astype(bf16)
        other = lax.ppermute(own, "c", SWAP)
        acts.append(jnp.concatenate([own, other], axis=0))
    for m in range(micros):
        recon = jnp.dot(acts[m], decoder, preferred_element_type=f32).astype(bf16)
        pieces = lax.all_to_all(recon.reshape(N_LAT, ROWS, -1), LAT, 0, 0)
        summed = jnp.sum(pieces.astype(f32), axis=0)
        mine = lax.dynamic_slice_in_dim(toks[m], lat * ROWS, ROWS, axis=0)
        residue = summed + dec_bias[None, :] - mine.astype(f32)
        err = (residue / MB_TOK).astype(bf16)
        errs.append(lax.all_to_all(jnp.broadcast_to(err[None], (N_LAT,) + err.shape), LAT, 0, 0).reshape(MB_TOK, -1))
    for m in range(micros):
        part = lax.dot_general(errs[m], decoder, (((1,), (1,)), ((), ())), preferred_element_type=f32).astype(bf16)
        pre_grad = jnp.where(gates[m] != 0, wid_sum(part), 0.0).astype(bf16)
        other = lax.ppermute(pre_grad, "c", SWAP)
        pres.append(jnp.concatenate([pre_grad, other], axis=0))
    tok = jnp.concatenate(toks, axis=0)
    act = jnp.concatenate(acts, axis=0)
    err = jnp.concatenate(errs, axis=0)
    pre = jnp.concatenate(pres, axis=0)
    rows = (((0,), (0,)), ((), ()))
    grad_enc = lax.dot_general(tok, pre, rows, preferred_element_type=f32)
    grad_dec = lax.dot_general(act, err, rows, preferred_element_type=f32)
    return grad_enc, grad_dec, jnp.sum(pre.astype(f32), axis=0), jnp.sum(err.astype(f32), axis=0)


def solution(mesh):
    fine = Mesh(mesh.devices.reshape(8, 4, 2, 2, 2), LAT + WID)
    in_specs = (P(None, None, WID), P(WID, LAT), P(LAT, WID), P(LAT), P(WID), P(None, None, LAT))
    out_specs = (P(WID, LAT), P(LAT, WID), P(LAT), P(WID))
    return jax.shard_map(shards, mesh=fine, in_specs=in_specs, out_specs=out_specs, check_vma=False)
```

```python
import jax
import jax.numpy as jnp
from jax import lax
from jax.experimental import pallas as pl
from jax.experimental.pallas import tpu as pltpu
from jax.sharding import Mesh
from jax.sharding import PartitionSpec as P

MB_TOK = 256
Q = 64
CHUNK = 2 * Q
LAT = ("z", "y", "xh")
WID = ("xl", "c")
FAR = ("z", "xh")
PEERS = 16
ROWS = CHUNK // PEERS
FIRST_LIMIT = 52
FIRST, LAST = (2, 3), (1, 0)
GROUPS = (FIRST, LAST)
ORDER = tuple(r for group in GROUPS for r in group)
SWAP = [(0, 1), (1, 0)]
f32, bf16, i32 = jnp.float32, jnp.bfloat16, jnp.int32
VMEM = pl.BlockSpec(memory_space=pltpu.VMEM)
SMEM = pl.BlockSpec(memory_space=pltpu.SMEM)
ANY = pl.BlockSpec(memory_space=pl.ANY)
TINY = pl.CostEstimate(flops=1, bytes_accessed=1, transcendentals=0)
DOWN = (((0,), (0,)), ((), ()))
ACROSS = (((1,), (1,)), ((), ()))


def call(kernel, outs, args, ids=None, after=(), scratch=(), limit=24):
    skip = len(after)

    def body(*refs):
        kernel(*refs[skip:])

    return pl.pallas_call(
        body,
        out_shape=[jax.ShapeDtypeStruct(s, t) for s, t in outs],
        in_specs=[ANY] * skip + ([] if ids is None else [SMEM]) + [VMEM] * len(args),
        out_specs=[VMEM] * len(outs),
        scratch_shapes=scratch,
        compiler_params=pltpu.CompilerParams(vmem_limit_bytes=limit << 20),
        cost_estimate=TINY,
    )(*after, *([] if ids is None else [ids]), *args)


def encode_first(ids, tokens, encoder, group):
    d, n = encoder.shape
    parts = 4
    rows = len(group) * Q
    order = [2 * r + h for h in (0, 1) for r in group]

    def kernel(ids_ref, tok_hbm, enc_hbm, keep_ref, send_ref, tok, enc, sems):
        pieces = [pl.ds(k * (d // parts), d // parts) for k in range(parts)]
        blocks = [pl.ds(k * (8 // parts), 8 // parts) for k in range(parts)]
        copies = [pltpu.make_async_copy(tok_hbm.at[at], tok.at[at], sems.at[k]) for k, at in enumerate(blocks)]
        copies += [pltpu.make_async_copy(enc_hbm.at[at], enc.at[at], sems.at[parts + k]) for k, at in enumerate(pieces)]
        for copy in copies:
            copy.start()
        for copy in copies:
            copy.wait()
        lhs = jnp.concatenate([tok[ids_ref[at]] for at in order], axis=0)
        for j in range(0, n, 256):
            out = jnp.dot(lhs, enc[:, j:j + 256], preferred_element_type=f32).astype(bf16)
            keep_ref[:, j:j + 256] = out[:rows]
            send_ref[:, j:j + 256] = out[rows:]

    return pl.pallas_call(
        kernel,
        out_shape=[jax.ShapeDtypeStruct(s, bf16) for s in ((rows, n), (rows, n), tokens.shape)],
        in_specs=[SMEM, ANY, ANY],
        out_specs=[VMEM] * 3,
        scratch_shapes=[pltpu.VMEM((d, n), bf16), pltpu.SemaphoreType.DMA((2 * parts,))],
        compiler_params=pltpu.CompilerParams(vmem_limit_bytes=FIRST_LIMIT << 20),
        cost_estimate=TINY,
    )(ids, tokens, encoder)


def encode(ids, tokens, encoder, groups):
    n = encoder.shape[1]
    order = [(2 * r + h, k, h) for k, group in enumerate(groups) for h in (0, 1) for r in group]
    sizes = [len(group) * Q for group in groups for h in (0, 1)]

    def kernel(ids_ref, tok_ref, enc_ref, *outs):
        lhs = jnp.concatenate([tok_ref[ids_ref[at]] for at, _, _ in order], axis=0)
        for j in range(0, n, 256):
            out = jnp.dot(lhs, enc_ref[:, j:j + 256], preferred_element_type=f32).astype(bf16)
            at = 0
            for size, ref in zip(sizes, outs):
                ref[:, j:j + 256] = out[at:at + size]
                at += size

    return call(kernel, [((size, n), bf16) for size in sizes], (tokens, encoder), ids)


def gates(ids, masks, after):
    n = masks.shape[-1]

    def kernel(ids_ref, mask_ref, *outs):
        shift = lax.broadcasted_iota(i32, (16, n), 0)
        for group, out_ref in zip(GROUPS, outs):
            for k, r in enumerate(group):
                words = mask_ref[ids_ref[2 * r]]
                for w in range(Q // 16):
                    bit = jnp.right_shift(jnp.broadcast_to(words[w:w + 1], (16, n)), shift) & 1
                    out_ref[k * Q + 16 * w:k * Q + 16 * w + 16] = bit.astype(f32).astype(bf16)

    return call(kernel, [((len(group) * Q, n), bf16) for group in GROUPS], (masks,), ids, after)


def activity(gate, chip, away, bias, after):
    def kernel(gate_ref, chip_ref, away_ref, bias_ref, out_ref):
        value = chip_ref[...].astype(f32) + away_ref[...].astype(f32) + bias_ref[...].reshape(1, -1)
        out_ref[...] = (value * gate_ref[...].astype(f32)).astype(bf16)

    return call(kernel, [(chip.shape, bf16)], (gate, chip, away, bias), None, after)[0]


def gradient(gate, chip, away, after=()):
    def kernel(gate_ref, chip_ref, away_ref, out_ref):
        value = chip_ref[...].astype(f32) + away_ref[...].astype(f32)
        out_ref[...] = (value * gate_ref[...].astype(f32)).astype(bf16)

    return call(kernel, [(chip.shape, bf16)], (gate, chip, away), None, after)[0]


def decode(own, dec_own, dec_other, after=()):
    n = dec_own.shape[1]
    count = own.shape[0] // Q

    def kernel(own_ref, dec_ref, oth_ref, *outs):
        for k, ref in enumerate((dec_ref, oth_ref)):
            for j in range(0, n, 256):
                at = slice(j, min(j + 256, n))
                out = jnp.dot(own_ref[...], ref[:, at], preferred_element_type=f32).astype(bf16)
                for q, out_ref in enumerate(outs):
                    out_ref[k * Q:k * Q + Q, at] = out[q * Q:q * Q + Q]

    return call(kernel, [((CHUNK, n), bf16)] * count, (own, dec_own, dec_other), None, after)


def bases(ids, tokens, bias):
    shape = ((ROWS, bias.shape[0]), f32)

    def kernel(ids_ref, tok_ref, bias_ref, own_ref, send_ref):
        bias = bias_ref[...].reshape(1, -1)
        own_ref[...] = bias - tok_ref[ids_ref[8]].astype(f32)
        send_ref[...] = bias - tok_ref[ids_ref[9]].astype(f32)

    return call(kernel, [shape, shape], (tokens, bias), ids)


def error(ids, pieces, own, other):
    def kernel(ids_ref, piece_ref, own_ref, other_ref, out_ref):
        total = jnp.where(ids_ref[10] == 0, own_ref[...], other_ref[...])
        for k in range(PEERS):
            total = total + piece_ref[k].astype(f32)
        value = (total / MB_TOK).astype(bf16)
        for k in range(PEERS):
            out_ref[k] = value

    return call(kernel, [(pieces.shape, bf16)], (pieces, own, other), ids)[0]


def back(errs, dec_own, dec_other, after=()):
    n = dec_own.shape[1]
    count = len(errs)

    def kernel(*refs):
        dec_ref, oth_ref, out_ref = refs[count:]
        own = jnp.concatenate([ref[:Q] for ref in refs[:count]], axis=0)
        other = jnp.concatenate([ref[Q:] for ref in refs[:count]], axis=0)
        out = jnp.dot(own, dec_ref[...], preferred_element_type=f32)
        out = out + jnp.dot(other, oth_ref[...], preferred_element_type=f32)
        out_ref[...] = out.astype(bf16)

    return call(kernel, [((count * Q, n), bf16)], (*errs, dec_own, dec_other), None, after)[0]


def flipped(x, after):
    def kernel(x_ref, out_ref, same_ref):
        for j in range(0, x.shape[0], 256):
            block = x_ref[j:j + 256]
            out_ref[:, j:j + 256] = block.T
            same_ref[j:j + 256] = block

    return call(kernel, [(x.shape[::-1], bf16), (x.shape, bf16)], (x,), None, after)


def turned(ids, tokens, after):
    d = tokens.shape[-1]

    def kernel(ids_ref, tok_ref, out_ref):
        at = 0
        for h in (0, 1):
            for group in (ORDER[:2], ORDER[2:]):
                pair = jnp.concatenate([tok_ref[ids_ref[2 * r + h]] for r in group], axis=0)
                out_ref[:, at:at + CHUNK] = pair.T
                at += CHUNK

    return call(kernel, [((d, 4 * CHUNK), bf16)], (tokens,), ids, after)[0]


def decoder_grad(owns, others, errs, err_others, after):
    n, d = others.shape[1], errs[0].shape[1]
    tile = 256
    skip = len(after)
    rows = len(ORDER) * Q

    def kernel(*refs):
        a0, a1, a2, e0, e1, e2, e3, other, out_ref, sum_ref, done_ref, err_ref = refs[skip:]

        @pl.when(pl.program_id(0) == 0)
        def _():
            e = (e0, e1, e2, e3)
            for k, r in enumerate(ORDER):
                err_ref[k * Q:k * Q + Q] = e[r][:Q]
            err_ref[rows:] = other[...]
            sum_ref[...] = jnp.sum(err_ref[...].astype(f32), axis=0)
            done_ref[...] = jnp.zeros_like(done_ref)

        lhs = jnp.concatenate([a0[...], a1[...], a2[...]], axis=0)
        out_ref[...] = lax.dot_general(lhs, err_ref[...], DOWN, preferred_element_type=f32)

    acts = (*owns, others)
    return pl.pallas_call(
        kernel,
        grid=(n // tile,),
        in_specs=[ANY] * skip
        + [pl.BlockSpec((act.shape[0], tile), lambda i: (0, i)) for act in acts]
        + [pl.BlockSpec((CHUNK, d), lambda i: (0, 0))] * 4
        + [pl.BlockSpec((rows, d), lambda i: (0, 0))],
        out_specs=[
            pl.BlockSpec((tile, d), lambda i: (i, 0)),
            pl.BlockSpec((d,), lambda i: (0,)),
            pl.BlockSpec((8, 128), lambda i: (0, 0)),
        ],
        out_shape=[jax.ShapeDtypeStruct((n, d), f32), jax.ShapeDtypeStruct((d,), f32), jax.ShapeDtypeStruct((8, 128), f32)],
        scratch_shapes=[pltpu.VMEM((2 * rows, d), bf16)],
        compiler_params=pltpu.CompilerParams(vmem_limit_bytes=24 << 20),
        cost_estimate=TINY,
    )(*after, *acts, *errs, err_others)


def encoder_grad(tok_t, pres):
    d, n = tok_t.shape[0], pres[0].shape[1]
    parts = 7
    tile = d // parts
    count = len(pres)

    def kernel(t_ref, *refs):
        out_hbm, sum_ref, out, sems = refs[count:]
        pre = jnp.concatenate([ref[...] for ref in refs[:count]], axis=0)
        copies = []
        for k in range(parts):
            rows = pl.ds(k * tile, tile)
            out[rows] = jnp.dot(t_ref[rows], pre, preferred_element_type=f32)
            copies.append(pltpu.make_async_copy(out.at[rows], out_hbm.at[rows], sems.at[k]))
            copies[-1].start()
        sum_ref[...] = jnp.dot(jnp.ones((16, 4 * CHUNK), bf16), pre, preferred_element_type=f32)[0]
        for copy in copies:
            copy.wait()

    return pl.pallas_call(
        kernel,
        in_specs=[VMEM] * (1 + count),
        out_specs=[ANY, VMEM],
        out_shape=[jax.ShapeDtypeStruct((d, n), f32), jax.ShapeDtypeStruct((n,), f32)],
        scratch_shapes=[pltpu.VMEM((d, n), f32), pltpu.SemaphoreType.DMA((parts,))],
        compiler_params=pltpu.CompilerParams(vmem_limit_bytes=24 << 20),
        cost_estimate=TINY,
    )(tok_t, *pres)


def swap(x, axis, name):
    with jax.named_scope(name):
        return lax.ppermute(x, axis, SWAP)


def partner(x, r, name):
    with jax.named_scope(name):
        return lax.ppermute(x, "y", [(i, i ^ r) for i in range(4)])


def add(a, b, after=()):
    def kernel(a_ref, b_ref, out_ref):
        out_ref[...] = (a_ref[...].astype(f32) + b_ref[...].astype(f32)).astype(bf16)

    return call(kernel, [(a.shape, bf16)], (a, b), None, after)[0]


def stacked(parts, after=()):
    rows = [x.shape[0] - at for x, at in parts]

    def kernel(*refs):
        at = 0
        for (_, start), size, ref in zip(parts, rows, refs):
            refs[-1][at:at + size] = ref[start:]
            at += size

    shape = ((sum(rows), parts[0][0].shape[1]), bf16)
    return call(kernel, [shape], [x for x, _ in parts], None, after)[0]


def add3(a, b, c):
    def kernel(a_ref, b_ref, c_ref, out_ref):
        out_ref[...] = a_ref[...].astype(f32) + b_ref[...].astype(f32) + c_ref[...].astype(f32)

    return call(kernel, [(a.shape, f32)], (a, b, c))[0]


def shards(tokens, encoder, decoder, enc_bias, dec_bias, masks):
    c = lax.axis_index("c")
    y = lax.axis_index("y")
    far = lax.axis_index(FAR)
    d = tokens.shape[-1]
    tokens = tokens.reshape(8, Q, d)
    masks = masks.reshape(8, Q // 16, -1)
    groups = Q // ROWS
    k = jnp.arange(11, dtype=i32)
    ids = (y ^ (k >> 1)) * 2 + (c ^ (k & 1))
    ids = jnp.where(k >= 8, (y * 2 + (c ^ (k & 1))) * groups + far % groups, ids)
    ids = jnp.where(k == 10, far // groups, ids)

    keep0, send0, tokens = encode_first(ids, tokens, encoder, FIRST)
    got0 = swap(send0, "c", "got0")
    keep1, send1 = encode(ids, tokens, encoder, (LAST,))
    got1 = swap(send1, "c", "got1")
    chip0 = add(keep0, got0)
    away0 = swap(chip0, "xl", "away0")
    gate0, gate1 = gates(ids, masks, [chip0])
    tok_t = turned(ids, tokens, [chip0])
    chip1 = add(keep1, got1, [tok_t, gate0])
    away1 = swap(chip1, "xl", "away1")
    decoder2 = swap(decoder, "c", "decoder2")
    base, base_send = bases(ids, tokens.reshape(-1, ROWS, d), dec_bias)
    base2 = swap(base_send, "c", "base2")
    dec_t, dec = flipped(decoder, [chip1])
    dec_t2, dec2 = flipped(decoder2, [chip1])
    act0 = activity(gate0, chip0, away0, enc_bias, [dec_t, dec_t2, base2])
    r2, r3 = decode(act0, dec, dec2)
    g2, g3 = partner(r2, 2, "g2"), partner(r3, 3, "g3")
    act1 = activity(gate1, chip1, away1, enc_bias, [r2])
    r1, r0 = decode(act1, dec, dec2)
    g1 = partner(r1, 1, "g1")
    total = add(add3(r0, g2, g3), g1)
    pieces = lax.all_to_all(total.reshape(PEERS, ROWS, d), FAR, 0, 0)
    copies = error(ids, pieces, base, base2)
    e0 = lax.all_to_all(copies, FAR, 0, 0).reshape(CHUNK, d)
    e1, e3, e2 = partner(e0, 1, "e1"), partner(e0, 3, "e3"), partner(e0, 2, "e2")
    part1 = back([e1, e0], dec_t, dec_t2)
    away1 = swap(part1, "xl", "back1")
    part0 = back([e2, e3], dec_t, dec_t2, [part1])
    away0 = swap(part0, "xl", "back0")
    act_others = swap(stacked([(act0, 0), (act1, 0)], [e0]), "c", "act_others")
    err_others = swap(stacked([(e2, Q), (e3, Q), (e1, Q), (e0, Q)]), "c", "err_others")
    pre1 = gradient(gate1, part1, away1, [part0])
    pre1o = swap(pre1, "c", "pre1o")
    grad_dec, dec_sum, done = decoder_grad((act0, act1), act_others, (e0, e1, e2, e3), err_others, [part0])
    pre0 = gradient(gate0, part0, away0, [done, pre1])
    pre0o = swap(pre0, "c", "pre0o")
    grad_enc, enc_sum = encoder_grad(tok_t, [pre0, pre1, pre0o, pre1o])
    return grad_enc, grad_dec, enc_sum, dec_sum


def solution(mesh):
    fine = Mesh(mesh.devices.reshape(8, 4, 2, 2, 2), LAT + WID)
    in_specs = (P(None, None, WID), P(WID, LAT), P(LAT, WID), P(LAT), P(WID), P(None, None, LAT))
    out_specs = (P(WID, LAT), P(LAT, WID), P(LAT), P(WID))
    return jax.shard_map(shards, mesh=fine, in_specs=in_specs, out_specs=out_specs, check_vma=False)
```

```python
import jax
import jax.numpy as jnp
from jax import lax
from jax.experimental import pallas as pl
from jax.experimental.pallas import tpu as pltpu
from jax.sharding import Mesh
from jax.sharding import PartitionSpec as P

MB_TOK = 256
Q = 64
CHUNK = 2 * Q
LAT = ("z", "y", "xh")
WID = ("xl", "c")
FAR = ("z", "xh")
PEERS = 16
ROWS = CHUNK // PEERS
FIRST_LIMIT = 52
FIRST, LAST = (2, 3), (1, 0)
GROUPS = (FIRST, LAST)
ORDER = tuple(r for group in GROUPS for r in group)
SWAP = [(0, 1), (1, 0)]
f32, bf16, i32 = jnp.float32, jnp.bfloat16, jnp.int32
VMEM = pl.BlockSpec(memory_space=pltpu.VMEM)
SMEM = pl.BlockSpec(memory_space=pltpu.SMEM)
ANY = pl.BlockSpec(memory_space=pl.ANY)
TINY = pl.CostEstimate(flops=1, bytes_accessed=1, transcendentals=0)
DOWN = (((0,), (0,)), ((), ()))
ACROSS = (((1,), (1,)), ((), ()))


def call(kernel, outs, args, ids=None, after=(), scratch=(), limit=24):
    skip = len(after)

    def body(*refs):
        kernel(*refs[skip:])

    return pl.pallas_call(
        body,
        out_shape=[jax.ShapeDtypeStruct(s, t) for s, t in outs],
        in_specs=[ANY] * skip + ([] if ids is None else [SMEM]) + [VMEM] * len(args),
        out_specs=[VMEM] * len(outs),
        scratch_shapes=scratch,
        compiler_params=pltpu.CompilerParams(vmem_limit_bytes=limit << 20),
        cost_estimate=TINY,
    )(*after, *([] if ids is None else [ids]), *args)


def encode_first(ids, tokens, encoder, group):
    d, n = encoder.shape
    parts = 4
    rows = len(group) * Q
    order = [2 * r + h for h in (0, 1) for r in group]

    def kernel(ids_ref, tok_hbm, enc_hbm, keep_ref, send_ref, tok, enc, sems):
        pieces = [pl.ds(k * (d // parts), d // parts) for k in range(parts)]
        blocks = [pl.ds(k * (8 // parts), 8 // parts) for k in range(parts)]
        copies = [pltpu.make_async_copy(tok_hbm.at[at], tok.at[at], sems.at[k]) for k, at in enumerate(blocks)]
        copies += [pltpu.make_async_copy(enc_hbm.at[at], enc.at[at], sems.at[parts + k]) for k, at in enumerate(pieces)]
        for copy in copies:
            copy.start()
        for copy in copies:
            copy.wait()
        lhs = jnp.concatenate([tok[ids_ref[at]] for at in order], axis=0)
        for j in range(0, n, 256):
            out = jnp.dot(lhs, enc[:, j:j + 256], preferred_element_type=f32).astype(bf16)
            keep_ref[:, j:j + 256] = out[:rows]
            send_ref[:, j:j + 256] = out[rows:]

    return pl.pallas_call(
        kernel,
        out_shape=[jax.ShapeDtypeStruct(s, bf16) for s in ((rows, n), (rows, n), tokens.shape)],
        in_specs=[SMEM, ANY, ANY],
        out_specs=[VMEM] * 3,
        scratch_shapes=[pltpu.VMEM((d, n), bf16), pltpu.SemaphoreType.DMA((2 * parts,))],
        compiler_params=pltpu.CompilerParams(vmem_limit_bytes=FIRST_LIMIT << 20),
        cost_estimate=TINY,
    )(ids, tokens, encoder)


def encode(ids, tokens, encoder, groups):
    n = encoder.shape[1]
    order = [(2 * r + h, k, h) for k, group in enumerate(groups) for h in (0, 1) for r in group]
    sizes = [len(group) * Q for group in groups for h in (0, 1)]

    def kernel(ids_ref, tok_ref, enc_ref, *outs):
        lhs = jnp.concatenate([tok_ref[ids_ref[at]] for at, _, _ in order], axis=0)
        for j in range(0, n, 256):
            out = jnp.dot(lhs, enc_ref[:, j:j + 256], preferred_element_type=f32).astype(bf16)
            at = 0
            for size, ref in zip(sizes, outs):
                ref[:, j:j + 256] = out[at:at + size]
                at += size

    return call(kernel, [((size, n), bf16) for size in sizes], (tokens, encoder), ids)


def gates(ids, masks, after):
    n = masks.shape[-1]

    def kernel(ids_ref, mask_ref, *outs):
        shift = lax.broadcasted_iota(i32, (16, n), 0)
        for group, out_ref in zip(GROUPS, outs):
            for k, r in enumerate(group):
                words = mask_ref[ids_ref[2 * r]]
                for w in range(Q // 16):
                    bit = jnp.right_shift(jnp.broadcast_to(words[w:w + 1], (16, n)), shift) & 1
                    out_ref[k * Q + 16 * w:k * Q + 16 * w + 16] = bit.astype(f32).astype(bf16)

    return call(kernel, [((len(group) * Q, n), bf16) for group in GROUPS], (masks,), ids, after)


def activity(gate, chip, away, bias, after):
    def kernel(gate_ref, chip_ref, away_ref, bias_ref, out_ref):
        value = chip_ref[...].astype(f32) + away_ref[...].astype(f32) + bias_ref[...].reshape(1, -1)
        out_ref[...] = (value * gate_ref[...].astype(f32)).astype(bf16)

    return call(kernel, [(chip.shape, bf16)], (gate, chip, away, bias), None, after)[0]


def gradient(gate, chips, aways, after=()):
    count = len(chips)
    rows = chips[0].shape[0]

    def kernel(gate_ref, *refs):
        for k in range(count):
            at = slice(k * rows, k * rows + rows)
            value = refs[k][...].astype(f32) + refs[count + k][...].astype(f32)
            refs[-1][at] = (value * gate_ref[at].astype(f32)).astype(bf16)

    return call(kernel, [(gate.shape, bf16)], (gate, *chips, *aways), None, after)[0]


def decode(own, dec_own, dec_other, after=()):
    n = dec_own.shape[1]
    count = own.shape[0] // Q

    def kernel(own_ref, dec_ref, oth_ref, *outs):
        for k, ref in enumerate((dec_ref, oth_ref)):
            for j in range(0, n, 256):
                at = slice(j, min(j + 256, n))
                out = jnp.dot(own_ref[...], ref[:, at], preferred_element_type=f32).astype(bf16)
                for q, out_ref in enumerate(outs):
                    out_ref[k * Q:k * Q + Q, at] = out[q * Q:q * Q + Q]

    return call(kernel, [((CHUNK, n), bf16)] * count, (own, dec_own, dec_other), None, after)


def bases(ids, tokens, bias):
    shape = ((ROWS, bias.shape[0]), f32)

    def kernel(ids_ref, tok_ref, bias_ref, own_ref, send_ref):
        bias = bias_ref[...].reshape(1, -1)
        own_ref[...] = bias - tok_ref[ids_ref[8]].astype(f32)
        send_ref[...] = bias - tok_ref[ids_ref[9]].astype(f32)

    return call(kernel, [shape, shape], (tokens, bias), ids)


def error(ids, pieces, own, other):
    def kernel(ids_ref, piece_ref, own_ref, other_ref, out_ref):
        total = jnp.where(ids_ref[10] == 0, own_ref[...], other_ref[...])
        for k in range(PEERS):
            total = total + piece_ref[k].astype(f32)
        value = (total / MB_TOK).astype(bf16)
        for k in range(PEERS):
            out_ref[k] = value

    return call(kernel, [(pieces.shape, bf16)], (pieces, own, other), ids)[0]


def back(errs, dec_own, dec_other, sizes, after=()):
    n = dec_own.shape[1]
    count = len(errs)

    def kernel(*refs):
        dec_ref, oth_ref = refs[count:count + 2]
        own = jnp.concatenate([ref[:Q] for ref in refs[:count]], axis=0)
        other = jnp.concatenate([ref[Q:] for ref in refs[:count]], axis=0)
        out = jnp.dot(own, dec_ref[...], preferred_element_type=f32)
        out = out + jnp.dot(other, oth_ref[...], preferred_element_type=f32)
        out = out.astype(bf16)
        at = 0
        for size, ref in zip(sizes, refs[count + 2:]):
            ref[...] = out[at:at + size * Q]
            at += size * Q

    return call(kernel, [((size * Q, n), bf16) for size in sizes], (*errs, dec_own, dec_other), None, after)


def flipped(x, after):
    def kernel(x_ref, out_ref, same_ref):
        for j in range(0, x.shape[0], 256):
            block = x_ref[j:j + 256]
            out_ref[:, j:j + 256] = block.T
            same_ref[j:j + 256] = block

    return call(kernel, [(x.shape[::-1], bf16), (x.shape, bf16)], (x,), None, after)


def turned(ids, tokens, after):
    d = tokens.shape[-1]

    def kernel(ids_ref, tok_ref, out_ref):
        at = 0
        for h in (0, 1):
            for group in (ORDER[:2], ORDER[2:]):
                pair = jnp.concatenate([tok_ref[ids_ref[2 * r + h]] for r in group], axis=0)
                out_ref[:, at:at + CHUNK] = pair.T
                at += CHUNK

    return call(kernel, [((d, 4 * CHUNK), bf16)], (tokens,), ids, after)[0]


def columns(parts, n, after):
    rows = sum(x.shape[0] for x in parts)
    shape = (n, rows)

    def kernel(*refs):
        whole = jnp.concatenate([ref[:, :n] for ref in refs[:-1]], axis=0)
        for at in range(0, rows, CHUNK):
            refs[-1][:, at:at + CHUNK] = whole[at:at + CHUNK].T

    return call(kernel, [(shape, bf16)], parts, None, after)[0]


def product(lefts, parts, after=()):
    d, n = lefts[0].shape[0], parts[0][0].shape[1]
    pieces = d // CHUNK
    count = len(parts)
    skip = len(after)
    wide = len(lefts)

    def kernel(*refs):
        left_refs, refs = refs[skip:skip + wide], refs[skip + wide:]
        out_hbm, sum_ref, done_ref, out, sems = refs[count:]
        right = jnp.concatenate([ref[:rows, -n:] for ref, (_, rows) in zip(refs, parts)], axis=0)
        copies = []
        for k in range(pieces):
            rows = pl.ds(k * CHUNK, CHUNK)
            left = jnp.concatenate([ref[rows] for ref in left_refs], axis=1)
            out[rows] = jnp.dot(left, right, preferred_element_type=f32)
            copies.append(pltpu.make_async_copy(out.at[rows], out_hbm.at[rows], sems.at[k]))
            copies[-1].start()
        sum_ref[...] = jnp.dot(jnp.ones((16, right.shape[0]), bf16), right, preferred_element_type=f32)[0]
        done_ref[...] = jnp.zeros_like(done_ref)
        for copy in copies:
            copy.wait()

    return pl.pallas_call(
        kernel,
        in_specs=[ANY] * skip + [VMEM] * (wide + count),
        out_specs=[ANY, VMEM, VMEM],
        out_shape=[jax.ShapeDtypeStruct(s, f32) for s in ((d, n), (n,), (8, 128))],
        scratch_shapes=[pltpu.VMEM((d, n), f32), pltpu.SemaphoreType.DMA((pieces,))],
        compiler_params=pltpu.CompilerParams(vmem_limit_bytes=24 << 20),
        cost_estimate=TINY,
    )(*after, *lefts, *[x for x, _ in parts])


def swap(x, axis, name):
    with jax.named_scope(name):
        return lax.ppermute(x, axis, SWAP)


def partner(x, r, name):
    with jax.named_scope(name):
        return lax.ppermute(x, "y", [(i, i ^ r) for i in range(4)])


def add(a, b, after=()):
    def kernel(a_ref, b_ref, out_ref):
        out_ref[...] = (a_ref[...].astype(f32) + b_ref[...].astype(f32)).astype(bf16)

    return call(kernel, [(a.shape, bf16)], (a, b), None, after)[0]


def split(errs, acts, after):
    count = len(errs)
    n, d = acts[0][0].shape[1], errs[0][0].shape[1]

    def kernel(*refs):
        for k in range(count):
            refs[2 * count + k][:, :n] = refs[count + k][acts[k][1]:acts[k][1] + Q]
            refs[2 * count + k][:, n:] = refs[k][errs[k][1]:errs[k][1] + Q]

    args = [x for x, _ in errs] + [x for x, _ in acts]
    return call(kernel, [((Q, n + d), bf16)] * count, args, None, after)


def add3(a, b, c):
    def kernel(a_ref, b_ref, c_ref, out_ref):
        out_ref[...] = a_ref[...].astype(f32) + b_ref[...].astype(f32) + c_ref[...].astype(f32)

    return call(kernel, [(a.shape, f32)], (a, b, c))[0]


def shards(tokens, encoder, decoder, enc_bias, dec_bias, masks):
    c = lax.axis_index("c")
    y = lax.axis_index("y")
    far = lax.axis_index(FAR)
    d = tokens.shape[-1]
    tokens = tokens.reshape(8, Q, d)
    masks = masks.reshape(8, Q // 16, -1)
    groups = Q // ROWS
    k = jnp.arange(11, dtype=i32)
    ids = (y ^ (k >> 1)) * 2 + (c ^ (k & 1))
    ids = jnp.where(k >= 8, (y * 2 + (c ^ (k & 1))) * groups + far % groups, ids)
    ids = jnp.where(k == 10, far // groups, ids)

    keep0, send0, tokens = encode_first(ids, tokens, encoder, FIRST)
    got0 = swap(send0, "c", "got0")
    keep1, send1 = encode(ids, tokens, encoder, (LAST,))
    got1 = swap(send1, "c", "got1")
    chip0 = add(keep0, got0)
    away0 = swap(chip0, "xl", "away0")
    gate0, gate1 = gates(ids, masks, [chip0])
    tok_t = turned(ids, tokens, [chip0])
    chip1 = add(keep1, got1, [tok_t, gate0])
    away1 = swap(chip1, "xl", "away1")
    decoder2 = swap(decoder, "c", "decoder2")
    base, base_send = bases(ids, tokens.reshape(-1, ROWS, d), dec_bias)
    base2 = swap(base_send, "c", "base2")
    dec_t, dec = flipped(decoder, [chip1])
    dec_t2, dec2 = flipped(decoder2, [chip1])
    act0 = activity(gate0, chip0, away0, enc_bias, [dec_t, dec_t2, base2])
    r2, r3 = decode(act0, dec, dec2)
    g2, g3 = partner(r2, 2, "g2"), partner(r3, 3, "g3")
    act1 = activity(gate1, chip1, away1, enc_bias, [r2])
    r1, r0 = decode(act1, dec, dec2)
    g1 = partner(r1, 1, "g1")
    total = add(add3(r0, g2, g3), g1)
    pieces = lax.all_to_all(total.reshape(PEERS, ROWS, d), FAR, 0, 0)
    copies = error(ids, pieces, base, base2)
    e0 = lax.all_to_all(copies, FAR, 0, 0).reshape(CHUNK, d)
    e1, e3, e2 = partner(e0, 1, "e1"), partner(e0, 3, "e3"), partner(e0, 2, "e2")
    part1 = back([e1, e0], dec_t, dec_t2, [1, 1])
    away1 = [swap(part, "xl", "back1") for part in part1]
    part0 = back([e2, e3], dec_t, dec_t2, [2], part1[:1])
    away0 = [swap(part, "xl", "back0") for part in part0]
    act_own = columns([act0, act1], act0.shape[1], part0)
    moved = split([(e2, Q), (e3, Q), (e1, Q), (e0, Q)], [(act0, 0), (act0, Q), (act1, 0), (act1, Q)], [act_own])
    moved = [swap(x, "c", "moved") for x in moved]
    pre1 = gradient(gate1, part1, away1, [act_own])
    pre1o = swap(pre1, "c", "pre1o")
    act_other = columns(moved, act0.shape[1], [pre1])
    errs = [(e2, Q), (e3, Q), (e1, Q), (e0, Q)] + [(x, Q) for x in moved]
    pre0 = gradient(gate0, part0, away0, [act_other])
    pre0o = swap(pre0, "c", "pre0o")
    grad_dec, dec_sum, done = product([act_own, act_other], errs, [pre0])
    grad_enc, enc_sum, _ = product([tok_t], [(x, CHUNK) for x in (pre0, pre1, pre0o, pre1o)], [done])
    return grad_enc, grad_dec, enc_sum, dec_sum


def solution(mesh):
    fine = Mesh(mesh.devices.reshape(8, 4, 2, 2, 2), LAT + WID)
    in_specs = (P(None, None, WID), P(WID, LAT), P(LAT, WID), P(LAT), P(WID), P(None, None, LAT))
    out_specs = (P(WID, LAT), P(LAT, WID), P(LAT), P(WID))
    return jax.shard_map(shards, mesh=fine, in_specs=in_specs, out_specs=out_specs, check_vma=False)
```

```python
import jax
import jax.numpy as jnp
from jax import lax
from jax.experimental import pallas as pl
from jax.experimental.pallas import tpu as pltpu
from jax.sharding import Mesh
from jax.sharding import PartitionSpec as P

MB_TOK = 256
Q = 64
CHUNK = 2 * Q
LAT = ("z", "y", "xh")
WID = ("xl", "c")
FAR = ("xh", "z")
PEERS = 16
ROWS = CHUNK // PEERS
FIRST_LIMIT = 52
FIRST, LAST = (2, 3), (1, 0)
GROUPS = (FIRST, LAST)
ORDER = tuple(r for group in GROUPS for r in group)
SWAP = [(0, 1), (1, 0)]
f32, bf16, i32 = jnp.float32, jnp.bfloat16, jnp.int32
VMEM = pl.BlockSpec(memory_space=pltpu.VMEM)
SMEM = pl.BlockSpec(memory_space=pltpu.SMEM)
ANY = pl.BlockSpec(memory_space=pl.ANY)
TINY = pl.CostEstimate(flops=1, bytes_accessed=1, transcendentals=0)
DOWN = (((0,), (0,)), ((), ()))
ACROSS = (((1,), (1,)), ((), ()))


def call(kernel, outs, args, ids=None, after=(), scratch=(), limit=24):
    skip = len(after)

    def body(*refs):
        kernel(*refs[skip:])

    return pl.pallas_call(
        body,
        out_shape=[jax.ShapeDtypeStruct(s, t) for s, t in outs],
        in_specs=[ANY] * skip + ([] if ids is None else [SMEM]) + [VMEM] * len(args),
        out_specs=[VMEM] * len(outs),
        scratch_shapes=scratch,
        compiler_params=pltpu.CompilerParams(vmem_limit_bytes=limit << 20),
        cost_estimate=TINY,
    )(*after, *([] if ids is None else [ids]), *args)


def encode_first(ids, tokens, encoder, group):
    d, n = encoder.shape
    parts = 4
    rows = len(group) * Q
    order = [2 * r + h for h in (0, 1) for r in group]

    def kernel(ids_ref, tok_hbm, enc_hbm, keep_ref, send_ref, tok, enc, sems):
        pieces = [pl.ds(k * (d // parts), d // parts) for k in range(parts)]
        blocks = [pl.ds(k * (8 // parts), 8 // parts) for k in range(parts)]
        copies = [pltpu.make_async_copy(tok_hbm.at[at], tok.at[at], sems.at[k]) for k, at in enumerate(blocks)]
        copies += [pltpu.make_async_copy(enc_hbm.at[at], enc.at[at], sems.at[parts + k]) for k, at in enumerate(pieces)]
        for copy in copies:
            copy.start()
        for copy in copies:
            copy.wait()
        lhs = jnp.concatenate([tok[ids_ref[at]] for at in order], axis=0)
        for j in range(0, n, 256):
            out = jnp.dot(lhs, enc[:, j:j + 256], preferred_element_type=f32).astype(bf16)
            keep_ref[:, j:j + 256] = out[:rows]
            send_ref[:, j:j + 256] = out[rows:]

    return pl.pallas_call(
        kernel,
        out_shape=[jax.ShapeDtypeStruct(s, bf16) for s in ((rows, n), (rows, n), tokens.shape)],
        in_specs=[SMEM, ANY, ANY],
        out_specs=[VMEM] * 3,
        scratch_shapes=[pltpu.VMEM((d, n), bf16), pltpu.SemaphoreType.DMA((2 * parts,))],
        compiler_params=pltpu.CompilerParams(vmem_limit_bytes=FIRST_LIMIT << 20),
        cost_estimate=TINY,
    )(ids, tokens, encoder)


def encode(ids, tokens, encoder, groups):
    n = encoder.shape[1]
    order = [(2 * r + h, k, h) for k, group in enumerate(groups) for h in (0, 1) for r in group]
    sizes = [len(group) * Q for group in groups for h in (0, 1)]

    def kernel(ids_ref, tok_ref, enc_ref, *outs):
        lhs = jnp.concatenate([tok_ref[ids_ref[at]] for at, _, _ in order], axis=0)
        for j in range(0, n, 256):
            out = jnp.dot(lhs, enc_ref[:, j:j + 256], preferred_element_type=f32).astype(bf16)
            at = 0
            for size, ref in zip(sizes, outs):
                ref[:, j:j + 256] = out[at:at + size]
                at += size

    return call(kernel, [((size, n), bf16) for size in sizes], (tokens, encoder), ids)


def gates(ids, masks, after):
    n = masks.shape[-1]

    def kernel(ids_ref, mask_ref, *outs):
        shift = lax.broadcasted_iota(i32, (16, n), 0)
        for group, out_ref in zip(GROUPS, outs):
            for k, r in enumerate(group):
                words = mask_ref[ids_ref[2 * r]]
                for w in range(Q // 16):
                    bit = jnp.right_shift(jnp.broadcast_to(words[w:w + 1], (16, n)), shift) & 1
                    out_ref[k * Q + 16 * w:k * Q + 16 * w + 16] = bit.astype(f32).astype(bf16)

    return call(kernel, [((len(group) * Q, n), bf16) for group in GROUPS], (masks,), ids, after)


def activity(gate, chip, away, bias, after):
    def kernel(gate_ref, chip_ref, away_ref, bias_ref, out_ref):
        value = chip_ref[...].astype(f32) + away_ref[...].astype(f32) + bias_ref[...].reshape(1, -1)
        out_ref[...] = (value * gate_ref[...].astype(f32)).astype(bf16)

    return call(kernel, [(chip.shape, bf16)], (gate, chip, away, bias), None, after)[0]


def gradient(gate, chips, aways, after=()):
    count = len(chips)
    rows = chips[0].shape[0]

    def kernel(gate_ref, *refs):
        for k in range(count):
            at = slice(k * rows, k * rows + rows)
            value = refs[k][...].astype(f32) + refs[count + k][...].astype(f32)
            refs[-1][at] = (value * gate_ref[at].astype(f32)).astype(bf16)

    return call(kernel, [(gate.shape, bf16)], (gate, *chips, *aways), None, after)[0]


def decode(own, dec_own, dec_other, after=()):
    n = dec_own.shape[1]
    count = own.shape[0] // Q

    def kernel(own_ref, dec_ref, oth_ref, *outs):
        for k, ref in enumerate((dec_ref, oth_ref)):
            for j in range(0, n, 256):
                at = slice(j, min(j + 256, n))
                out = jnp.dot(own_ref[...], ref[:, at], preferred_element_type=f32).astype(bf16)
                for q, out_ref in enumerate(outs):
                    out_ref[k * Q:k * Q + Q, at] = out[q * Q:q * Q + Q]

    return call(kernel, [((CHUNK, n), bf16)] * count, (own, dec_own, dec_other), None, after)


def bases(ids, tokens, bias):
    shape = ((ROWS, bias.shape[0]), f32)

    def kernel(ids_ref, tok_ref, bias_ref, own_ref, send_ref):
        bias = bias_ref[...].reshape(1, -1)
        own_ref[...] = bias - tok_ref[ids_ref[8]].astype(f32)
        send_ref[...] = bias - tok_ref[ids_ref[9]].astype(f32)

    return call(kernel, [shape, shape], (tokens, bias), ids)


def error(ids, pieces, own, other):
    def kernel(ids_ref, piece_ref, own_ref, other_ref, out_ref):
        total = jnp.where(ids_ref[10] == 0, own_ref[...], other_ref[...])
        for k in range(PEERS):
            total = total + piece_ref[k].astype(f32)
        value = (total / MB_TOK).astype(bf16)
        for k in range(PEERS):
            out_ref[k] = value

    return call(kernel, [(pieces.shape, bf16)], (pieces, own, other), ids)[0]


def back(errs, dec_own, dec_other, sizes, after=()):
    n = dec_own.shape[1]
    count = len(errs)

    def kernel(*refs):
        dec_ref, oth_ref = refs[count:count + 2]
        own = jnp.concatenate([ref[:Q] for ref in refs[:count]], axis=0)
        other = jnp.concatenate([ref[Q:] for ref in refs[:count]], axis=0)
        out = jnp.dot(own, dec_ref[...], preferred_element_type=f32)
        out = out + jnp.dot(other, oth_ref[...], preferred_element_type=f32)
        out = out.astype(bf16)
        at = 0
        for size, ref in zip(sizes, refs[count + 2:]):
            ref[...] = out[at:at + size * Q]
            at += size * Q

    return call(kernel, [((size * Q, n), bf16) for size in sizes], (*errs, dec_own, dec_other), None, after)


def flipped(x, after):
    def kernel(x_ref, out_ref, same_ref):
        for j in range(0, x.shape[0], 256):
            block = x_ref[j:j + 256]
            out_ref[:, j:j + 256] = block.T
            same_ref[j:j + 256] = block

    return call(kernel, [(x.shape[::-1], bf16), (x.shape, bf16)], (x,), None, after)


def turned(ids, tokens, after):
    d = tokens.shape[-1]

    def kernel(ids_ref, tok_ref, out_ref):
        at = 0
        for h in (0, 1):
            for group in (ORDER[:2], ORDER[2:]):
                pair = jnp.concatenate([tok_ref[ids_ref[2 * r + h]] for r in group], axis=0)
                out_ref[:, at:at + CHUNK] = pair.T
                at += CHUNK

    return call(kernel, [((d, 4 * CHUNK), bf16)], (tokens,), ids, after)[0]


def columns(parts, n, after):
    rows = sum(x.shape[0] for x in parts)
    shape = (n, rows)

    def kernel(*refs):
        whole = jnp.concatenate([ref[:, :n] for ref in refs[:-1]], axis=0)
        for at in range(0, rows, CHUNK):
            refs[-1][:, at:at + CHUNK] = whole[at:at + CHUNK].T

    return call(kernel, [(shape, bf16)], parts, None, after)[0]


def product(lefts, parts, after=()):
    d, n = lefts[0].shape[0], parts[0][0].shape[1]
    pieces = d // CHUNK
    count = len(parts)
    skip = len(after)
    wide = len(lefts)

    def kernel(*refs):
        left_refs, refs = refs[skip:skip + wide], refs[skip + wide:]
        out_hbm, sum_ref, done_ref, out, sems = refs[count:]
        right = jnp.concatenate([ref[:rows, -n:] for ref, (_, rows) in zip(refs, parts)], axis=0)
        copies = []
        for k in range(pieces):
            rows = pl.ds(k * CHUNK, CHUNK)
            left = jnp.concatenate([ref[rows] for ref in left_refs], axis=1)
            out[rows] = jnp.dot(left, right, preferred_element_type=f32)
            copies.append(pltpu.make_async_copy(out.at[rows], out_hbm.at[rows], sems.at[k]))
            copies[-1].start()
        sum_ref[...] = jnp.dot(jnp.ones((16, right.shape[0]), bf16), right, preferred_element_type=f32)[0]
        done_ref[...] = jnp.zeros_like(done_ref)
        for copy in copies:
            copy.wait()

    return pl.pallas_call(
        kernel,
        in_specs=[ANY] * skip + [VMEM] * (wide + count),
        out_specs=[ANY, VMEM, VMEM],
        out_shape=[jax.ShapeDtypeStruct(s, f32) for s in ((d, n), (n,), (8, 128))],
        scratch_shapes=[pltpu.VMEM((d, n), f32), pltpu.SemaphoreType.DMA((pieces,))],
        compiler_params=pltpu.CompilerParams(vmem_limit_bytes=24 << 20),
        cost_estimate=TINY,
    )(*after, *lefts, *[x for x, _ in parts])


def swap(x, axis, name):
    with jax.named_scope(name):
        return lax.ppermute(x, axis, SWAP)


def partner(x, r, name):
    with jax.named_scope(name):
        return lax.ppermute(x, "y", [(i, i ^ r) for i in range(4)])


def add(a, b, after=()):
    def kernel(a_ref, b_ref, out_ref):
        out_ref[...] = (a_ref[...].astype(f32) + b_ref[...].astype(f32)).astype(bf16)

    return call(kernel, [(a.shape, bf16)], (a, b), None, after)[0]


def split(errs, acts, after):
    count = len(errs)
    n, d = acts[0][0].shape[1], errs[0][0].shape[1]

    def kernel(*refs):
        for k in range(count):
            refs[2 * count + k][:, :n] = refs[count + k][acts[k][1]:acts[k][1] + Q]
            refs[2 * count + k][:, n:] = refs[k][errs[k][1]:errs[k][1] + Q]

    args = [x for x, _ in errs] + [x for x, _ in acts]
    return call(kernel, [((Q, n + d), bf16)] * count, args, None, after)


def add3(a, b, c):
    def kernel(a_ref, b_ref, c_ref, out_ref):
        out_ref[...] = a_ref[...].astype(f32) + b_ref[...].astype(f32) + c_ref[...].astype(f32)

    return call(kernel, [(a.shape, f32)], (a, b, c))[0]


def shards(tokens, encoder, decoder, enc_bias, dec_bias, masks):
    c = lax.axis_index("c")
    y = lax.axis_index("y")
    far = lax.axis_index(FAR)
    d = tokens.shape[-1]
    tokens = tokens.reshape(8, Q, d)
    masks = masks.reshape(8, Q // 16, -1)
    groups = Q // ROWS
    k = jnp.arange(11, dtype=i32)
    ids = (y ^ (k >> 1)) * 2 + (c ^ (k & 1))
    ids = jnp.where(k >= 8, (y * 2 + (c ^ (k & 1))) * groups + far % groups, ids)
    ids = jnp.where(k == 10, far // groups, ids)

    keep0, send0, tokens = encode_first(ids, tokens, encoder, FIRST)
    got0 = swap(send0, "c", "got0")
    keep1, send1 = encode(ids, tokens, encoder, (LAST,))
    got1 = swap(send1, "c", "got1")
    chip0 = add(keep0, got0)
    away0 = swap(chip0, "xl", "away0")
    gate0, gate1 = gates(ids, masks, [chip0])
    tok_t = turned(ids, tokens, [chip0])
    chip1 = add(keep1, got1, [tok_t, gate0])
    away1 = swap(chip1, "xl", "away1")
    decoder2 = swap(decoder, "c", "decoder2")
    base, base_send = bases(ids, tokens.reshape(-1, ROWS, d), dec_bias)
    base2 = swap(base_send, "c", "base2")
    dec_t, dec = flipped(decoder, [chip1])
    dec_t2, dec2 = flipped(decoder2, [chip1])
    act0 = activity(gate0, chip0, away0, enc_bias, [dec_t, dec_t2, base2])
    r2, r3 = decode(act0, dec, dec2)
    g2, g3 = partner(r2, 2, "g2"), partner(r3, 3, "g3")
    act1 = activity(gate1, chip1, away1, enc_bias, [r2])
    r1, r0 = decode(act1, dec, dec2)
    g1 = partner(r1, 1, "g1")
    total = add(add3(r0, g2, g3), g1)
    pieces = lax.all_to_all(total.reshape(PEERS, ROWS, d), FAR, 0, 0)
    copies = error(ids, pieces, base, base2)
    e0 = lax.all_to_all(copies, FAR, 0, 0).reshape(CHUNK, d)
    e1, e3, e2 = partner(e0, 1, "e1"), partner(e0, 3, "e3"), partner(e0, 2, "e2")
    part1 = back([e1, e0], dec_t, dec_t2, [1, 1])
    away1 = [swap(part, "xl", "back1") for part in part1]
    part0 = back([e2, e3], dec_t, dec_t2, [2], part1[:1])
    away0 = [swap(part, "xl", "back0") for part in part0]
    act_own = columns([act0, act1], act0.shape[1], part0)
    moved = split([(e2, Q), (e3, Q), (e1, Q), (e0, Q)], [(act0, 0), (act0, Q), (act1, 0), (act1, Q)], [act_own])
    moved = [swap(x, "c", "moved") for x in moved]
    pre1 = gradient(gate1, part1, away1, [act_own])
    pre1o = swap(pre1, "c", "pre1o")
    act_other = columns(moved, act0.shape[1], [pre1])
    errs = [(e2, Q), (e3, Q), (e1, Q), (e0, Q)] + [(x, Q) for x in moved]
    pre0 = gradient(gate0, part0, away0, [act_other])
    pre0o = swap(pre0, "c", "pre0o")
    grad_dec, dec_sum, done = product([act_own, act_other], errs, [pre0])
    grad_enc, enc_sum, _ = product([tok_t], [(x, CHUNK) for x in (pre0, pre1, pre0o, pre1o)], [done])
    return grad_enc, grad_dec, enc_sum, dec_sum


def solution(mesh):
    fine = Mesh(mesh.devices.reshape(8, 4, 2, 2, 2), LAT + WID)
    in_specs = (P(None, None, WID), P(WID, LAT), P(LAT, WID), P(LAT), P(WID), P(None, None, LAT))
    out_specs = (P(WID, LAT), P(LAT, WID), P(LAT), P(WID))
    return jax.shard_map(shards, mesh=fine, in_specs=in_specs, out_specs=out_specs, check_vma=False)
```

```python
import jax
import jax.numpy as jnp
from jax import lax
from jax.experimental import pallas as pl
from jax.experimental.pallas import tpu as pltpu
from jax.sharding import Mesh
from jax.sharding import PartitionSpec as P

MB_TOK = 256
Q = 64
CHUNK = 2 * Q
LAT = ("za", "zb", "zc", "y", "xh")
WID = ("xl", "c")
FAR = ("xh", "za", "zc", "zb")
PEERS = 16
ROWS = CHUNK // PEERS
FIRST_LIMIT = 52
FIRST, LAST = (2, 3), (1, 0)
GROUPS = (FIRST, LAST)
ORDER = tuple(r for group in GROUPS for r in group)
SWAP = [(0, 1), (1, 0)]
f32, bf16, i32 = jnp.float32, jnp.bfloat16, jnp.int32
VMEM = pl.BlockSpec(memory_space=pltpu.VMEM)
SMEM = pl.BlockSpec(memory_space=pltpu.SMEM)
ANY = pl.BlockSpec(memory_space=pl.ANY)
TINY = pl.CostEstimate(flops=1, bytes_accessed=1, transcendentals=0)
DOWN = (((0,), (0,)), ((), ()))
ACROSS = (((1,), (1,)), ((), ()))


def call(kernel, outs, args, ids=None, after=(), scratch=(), limit=24):
    skip = len(after)

    def body(*refs):
        kernel(*refs[skip:])

    return pl.pallas_call(
        body,
        out_shape=[jax.ShapeDtypeStruct(s, t) for s, t in outs],
        in_specs=[ANY] * skip + ([] if ids is None else [SMEM]) + [VMEM] * len(args),
        out_specs=[VMEM] * len(outs),
        scratch_shapes=scratch,
        compiler_params=pltpu.CompilerParams(vmem_limit_bytes=limit << 20),
        cost_estimate=TINY,
    )(*after, *([] if ids is None else [ids]), *args)


def encode_first(ids, tokens, encoder, group):
    d, n = encoder.shape
    parts = 4
    rows = len(group) * Q
    order = [2 * r + h for h in (0, 1) for r in group]

    def kernel(ids_ref, tok_hbm, enc_hbm, keep_ref, send_ref, tok, enc, sems):
        pieces = [pl.ds(k * (d // parts), d // parts) for k in range(parts)]
        blocks = [pl.ds(k * (8 // parts), 8 // parts) for k in range(parts)]
        copies = [pltpu.make_async_copy(tok_hbm.at[at], tok.at[at], sems.at[k]) for k, at in enumerate(blocks)]
        copies += [pltpu.make_async_copy(enc_hbm.at[at], enc.at[at], sems.at[parts + k]) for k, at in enumerate(pieces)]
        for copy in copies:
            copy.start()
        for copy in copies:
            copy.wait()
        lhs = jnp.concatenate([tok[ids_ref[at]] for at in order], axis=0)
        for j in range(0, n, 256):
            out = jnp.dot(lhs, enc[:, j:j + 256], preferred_element_type=f32).astype(bf16)
            keep_ref[:, j:j + 256] = out[:rows]
            send_ref[:, j:j + 256] = out[rows:]

    return pl.pallas_call(
        kernel,
        out_shape=[jax.ShapeDtypeStruct(s, bf16) for s in ((rows, n), (rows, n), tokens.shape)],
        in_specs=[SMEM, ANY, ANY],
        out_specs=[VMEM] * 3,
        scratch_shapes=[pltpu.VMEM((d, n), bf16), pltpu.SemaphoreType.DMA((2 * parts,))],
        compiler_params=pltpu.CompilerParams(vmem_limit_bytes=FIRST_LIMIT << 20),
        cost_estimate=TINY,
    )(ids, tokens, encoder)


def encode(ids, tokens, encoder, groups):
    n = encoder.shape[1]
    order = [(2 * r + h, k, h) for k, group in enumerate(groups) for h in (0, 1) for r in group]
    sizes = [len(group) * Q for group in groups for h in (0, 1)]

    def kernel(ids_ref, tok_ref, enc_ref, *outs):
        lhs = jnp.concatenate([tok_ref[ids_ref[at]] for at, _, _ in order], axis=0)
        for j in range(0, n, 256):
            out = jnp.dot(lhs, enc_ref[:, j:j + 256], preferred_element_type=f32).astype(bf16)
            at = 0
            for size, ref in zip(sizes, outs):
                ref[:, j:j + 256] = out[at:at + size]
                at += size

    return call(kernel, [((size, n), bf16) for size in sizes], (tokens, encoder), ids)


def gates(ids, masks, after):
    n = masks.shape[-1]

    def kernel(ids_ref, mask_ref, *outs):
        shift = lax.broadcasted_iota(i32, (16, n), 0)
        for group, out_ref in zip(GROUPS, outs):
            for k, r in enumerate(group):
                words = mask_ref[ids_ref[2 * r]]
                for w in range(Q // 16):
                    bit = jnp.right_shift(jnp.broadcast_to(words[w:w + 1], (16, n)), shift) & 1
                    out_ref[k * Q + 16 * w:k * Q + 16 * w + 16] = bit.astype(f32).astype(bf16)

    return call(kernel, [((len(group) * Q, n), bf16) for group in GROUPS], (masks,), ids, after)


def activity(gate, chip, away, bias, after):
    def kernel(gate_ref, chip_ref, away_ref, bias_ref, out_ref):
        value = chip_ref[...].astype(f32) + away_ref[...].astype(f32) + bias_ref[...].reshape(1, -1)
        out_ref[...] = (value * gate_ref[...].astype(f32)).astype(bf16)

    return call(kernel, [(chip.shape, bf16)], (gate, chip, away, bias), None, after)[0]


def gradient(gate, chips, aways, after=()):
    count = len(chips)
    rows = chips[0].shape[0]

    def kernel(gate_ref, *refs):
        for k in range(count):
            at = slice(k * rows, k * rows + rows)
            value = refs[k][...].astype(f32) + refs[count + k][...].astype(f32)
            refs[-1][at] = (value * gate_ref[at].astype(f32)).astype(bf16)

    return call(kernel, [(gate.shape, bf16)], (gate, *chips, *aways), None, after)[0]


def decode(own, dec_own, dec_other, after=()):
    n = dec_own.shape[1]
    count = own.shape[0] // Q

    def kernel(own_ref, dec_ref, oth_ref, *outs):
        for k, ref in enumerate((dec_ref, oth_ref)):
            for j in range(0, n, 256):
                at = slice(j, min(j + 256, n))
                out = jnp.dot(own_ref[...], ref[:, at], preferred_element_type=f32).astype(bf16)
                for q, out_ref in enumerate(outs):
                    out_ref[k * Q:k * Q + Q, at] = out[q * Q:q * Q + Q]

    return call(kernel, [((CHUNK, n), bf16)] * count, (own, dec_own, dec_other), None, after)


def bases(ids, tokens, bias):
    shape = ((ROWS, bias.shape[0]), f32)

    def kernel(ids_ref, tok_ref, bias_ref, own_ref, send_ref):
        bias = bias_ref[...].reshape(1, -1)
        own_ref[...] = bias - tok_ref[ids_ref[8]].astype(f32)
        send_ref[...] = bias - tok_ref[ids_ref[9]].astype(f32)

    return call(kernel, [shape, shape], (tokens, bias), ids)


def error(ids, pieces, own, other):
    def kernel(ids_ref, piece_ref, own_ref, other_ref, out_ref):
        total = jnp.where(ids_ref[10] == 0, own_ref[...], other_ref[...])
        for k in range(PEERS):
            total = total + piece_ref[k].astype(f32)
        value = (total / MB_TOK).astype(bf16)
        for k in range(PEERS):
            out_ref[k] = value

    return call(kernel, [(pieces.shape, bf16)], (pieces, own, other), ids)[0]


def back(errs, dec_own, dec_other, sizes, after=()):
    n = dec_own.shape[1]
    count = len(errs)

    def kernel(*refs):
        dec_ref, oth_ref = refs[count:count + 2]
        own = jnp.concatenate([ref[:Q] for ref in refs[:count]], axis=0)
        other = jnp.concatenate([ref[Q:] for ref in refs[:count]], axis=0)
        out = jnp.dot(own, dec_ref[...], preferred_element_type=f32)
        out = out + jnp.dot(other, oth_ref[...], preferred_element_type=f32)
        out = out.astype(bf16)
        at = 0
        for size, ref in zip(sizes, refs[count + 2:]):
            ref[...] = out[at:at + size * Q]
            at += size * Q

    return call(kernel, [((size * Q, n), bf16) for size in sizes], (*errs, dec_own, dec_other), None, after)


def flipped(x, after):
    def kernel(x_ref, out_ref, same_ref):
        for j in range(0, x.shape[0], 256):
            block = x_ref[j:j + 256]
            out_ref[:, j:j + 256] = block.T
            same_ref[j:j + 256] = block

    return call(kernel, [(x.shape[::-1], bf16), (x.shape, bf16)], (x,), None, after)


def turned(ids, tokens, after):
    d = tokens.shape[-1]

    def kernel(ids_ref, tok_ref, out_ref):
        at = 0
        for h in (0, 1):
            for group in (ORDER[:2], ORDER[2:]):
                pair = jnp.concatenate([tok_ref[ids_ref[2 * r + h]] for r in group], axis=0)
                out_ref[:, at:at + CHUNK] = pair.T
                at += CHUNK

    return call(kernel, [((d, 4 * CHUNK), bf16)], (tokens,), ids, after)[0]


def columns(parts, n, after):
    rows = sum(x.shape[0] for x in parts)
    shape = (n, rows)

    def kernel(*refs):
        whole = jnp.concatenate([ref[:, :n] for ref in refs[:-1]], axis=0)
        for at in range(0, rows, CHUNK):
            refs[-1][:, at:at + CHUNK] = whole[at:at + CHUNK].T

    return call(kernel, [(shape, bf16)], parts, None, after)[0]


def product(lefts, parts, after=()):
    d, n = lefts[0].shape[0], parts[0][0].shape[1]
    pieces = d // CHUNK
    count = len(parts)
    skip = len(after)
    wide = len(lefts)

    def kernel(*refs):
        left_refs, refs = refs[skip:skip + wide], refs[skip + wide:]
        out_hbm, sum_ref, done_ref, out, sems = refs[count:]
        right = jnp.concatenate([ref[:rows, -n:] for ref, (_, rows) in zip(refs, parts)], axis=0)
        copies = []
        for k in range(pieces):
            rows = pl.ds(k * CHUNK, CHUNK)
            left = jnp.concatenate([ref[rows] for ref in left_refs], axis=1)
            out[rows] = jnp.dot(left, right, preferred_element_type=f32)
            copies.append(pltpu.make_async_copy(out.at[rows], out_hbm.at[rows], sems.at[k]))
            copies[-1].start()
        sum_ref[...] = jnp.dot(jnp.ones((16, right.shape[0]), bf16), right, preferred_element_type=f32)[0]
        done_ref[...] = jnp.zeros_like(done_ref)
        for copy in copies:
            copy.wait()

    return pl.pallas_call(
        kernel,
        in_specs=[ANY] * skip + [VMEM] * (wide + count),
        out_specs=[ANY, VMEM, VMEM],
        out_shape=[jax.ShapeDtypeStruct(s, f32) for s in ((d, n), (n,), (8, 128))],
        scratch_shapes=[pltpu.VMEM((d, n), f32), pltpu.SemaphoreType.DMA((pieces,))],
        compiler_params=pltpu.CompilerParams(vmem_limit_bytes=24 << 20),
        cost_estimate=TINY,
    )(*after, *lefts, *[x for x, _ in parts])


def swap(x, axis, name):
    with jax.named_scope(name):
        return lax.ppermute(x, axis, SWAP)


def partner(x, r, name):
    with jax.named_scope(name):
        return lax.ppermute(x, "y", [(i, i ^ r) for i in range(4)])


def add(a, b, after=()):
    def kernel(a_ref, b_ref, out_ref):
        out_ref[...] = (a_ref[...].astype(f32) + b_ref[...].astype(f32)).astype(bf16)

    return call(kernel, [(a.shape, bf16)], (a, b), None, after)[0]


def split(errs, acts, after):
    count = len(errs)
    n, d = acts[0][0].shape[1], errs[0][0].shape[1]

    def kernel(*refs):
        for k in range(count):
            refs[2 * count + k][:, :n] = refs[count + k][acts[k][1]:acts[k][1] + Q]
            refs[2 * count + k][:, n:] = refs[k][errs[k][1]:errs[k][1] + Q]

    args = [x for x, _ in errs] + [x for x, _ in acts]
    return call(kernel, [((Q, n + d), bf16)] * count, args, None, after)


def add3(a, b, c):
    def kernel(a_ref, b_ref, c_ref, out_ref):
        out_ref[...] = a_ref[...].astype(f32) + b_ref[...].astype(f32) + c_ref[...].astype(f32)

    return call(kernel, [(a.shape, f32)], (a, b, c))[0]


def shards(tokens, encoder, decoder, enc_bias, dec_bias, masks):
    c = lax.axis_index("c")
    y = lax.axis_index("y")
    far = lax.axis_index(FAR)
    d = tokens.shape[-1]
    tokens = tokens.reshape(8, Q, d)
    masks = masks.reshape(8, Q // 16, -1)
    groups = Q // ROWS
    k = jnp.arange(11, dtype=i32)
    ids = (y ^ (k >> 1)) * 2 + (c ^ (k & 1))
    ids = jnp.where(k >= 8, (y * 2 + (c ^ (k & 1))) * groups + far % groups, ids)
    ids = jnp.where(k == 10, far // groups, ids)

    keep0, send0, tokens = encode_first(ids, tokens, encoder, FIRST)
    got0 = swap(send0, "c", "got0")
    keep1, send1 = encode(ids, tokens, encoder, (LAST,))
    got1 = swap(send1, "c", "got1")
    chip0 = add(keep0, got0)
    away0 = swap(chip0, "xl", "away0")
    gate0, gate1 = gates(ids, masks, [chip0])
    tok_t = turned(ids, tokens, [chip0])
    chip1 = add(keep1, got1, [tok_t, gate0])
    away1 = swap(chip1, "xl", "away1")
    decoder2 = swap(decoder, "c", "decoder2")
    base, base_send = bases(ids, tokens.reshape(-1, ROWS, d), dec_bias)
    base2 = swap(base_send, "c", "base2")
    dec_t, dec = flipped(decoder, [chip1])
    dec_t2, dec2 = flipped(decoder2, [chip1])
    act0 = activity(gate0, chip0, away0, enc_bias, [dec_t, dec_t2, base2])
    r2, r3 = decode(act0, dec, dec2)
    g2, g3 = partner(r2, 2, "g2"), partner(r3, 3, "g3")
    act1 = activity(gate1, chip1, away1, enc_bias, [r2])
    r1, r0 = decode(act1, dec, dec2)
    g1 = partner(r1, 1, "g1")
    total = add(add3(r0, g2, g3), g1)
    pieces = lax.all_to_all(total.reshape(PEERS, ROWS, d), FAR, 0, 0)
    copies = error(ids, pieces, base, base2)
    e0 = lax.all_to_all(copies, FAR, 0, 0).reshape(CHUNK, d)
    e1, e3, e2 = partner(e0, 1, "e1"), partner(e0, 3, "e3"), partner(e0, 2, "e2")
    part1 = back([e1, e0], dec_t, dec_t2, [1, 1])
    away1 = [swap(part, "xl", "back1") for part in part1]
    part0 = back([e2, e3], dec_t, dec_t2, [2], part1[:1])
    away0 = [swap(part, "xl", "back0") for part in part0]
    act_own = columns([act0, act1], act0.shape[1], part0)
    moved = split([(e2, Q), (e3, Q), (e1, Q), (e0, Q)], [(act0, 0), (act0, Q), (act1, 0), (act1, Q)], [act_own])
    moved = [swap(x, "c", "moved") for x in moved]
    pre1 = gradient(gate1, part1, away1, [act_own])
    pre1o = swap(pre1, "c", "pre1o")
    act_other = columns(moved, act0.shape[1], [pre1])
    errs = [(e2, Q), (e3, Q), (e1, Q), (e0, Q)] + [(x, Q) for x in moved]
    pre0 = gradient(gate0, part0, away0, [act_other])
    pre0o = swap(pre0, "c", "pre0o")
    grad_dec, dec_sum, done = product([act_own, act_other], errs, [pre0])
    grad_enc, enc_sum, _ = product([tok_t], [(x, CHUNK) for x in (pre0, pre1, pre0o, pre1o)], [done])
    return grad_enc, grad_dec, enc_sum, dec_sum


def solution(mesh):
    fine = Mesh(mesh.devices.reshape(2, 2, 2, 4, 2, 2, 2), LAT + WID)
    in_specs = (P(None, None, WID), P(WID, LAT), P(LAT, WID), P(LAT), P(WID), P(None, None, LAT))
    out_specs = (P(WID, LAT), P(LAT, WID), P(LAT), P(WID))
    return jax.shard_map(shards, mesh=fine, in_specs=in_specs, out_specs=out_specs, check_vma=False)
```
